32 devices in a mesh: tm: 16 (over z, y, x), row: 2 (over core).
Axes of the slice: x: 2, y: 2, z: 4, core: 2. Of those that a mesh axis runs over, the one named last changes fastest.
Arguments:
- transition: float32 [1024, 1024], P('row'), may hold values from -1 to 1, as said below
- gain_fwd: float32 [1024, 1024], P(None, 'row'), may hold values from -0.0234375 to 0.0234375
- gain_bwd: float32 [1024, 1024], P(None, 'row'), may hold values from -0.0234375 to 0.0234375
- blend: float32 [1024, 1024], P(None, 'row'), may hold values from -0.1875 to 0.1875
- prior_state: float32 [1024], replicated, may hold values from -6 to 6
- final_state: float32 [1024], replicated, may hold values from -6 to 6
- obs_index: int32 [512, 128], P('tm'), may hold values from 0 to 1023
- obs_visible: int32 [512, 128], P('tm'), may hold values 0 or 1
- obs_value: float32 [512, 128], P('tm'), may hold values from -6 to 6
Outputs:
- smoothed: float32 [512, 1024], P('tm', 'row')
The draws below stay inside these ranges and needn't reach their ends.
Inputs may be any that keep to these rules, and one draw needn't show every extreme that they name: `transition`: symmetric; every eigenvalue lies strictly between 0 and 1.
All inputs are finite; a program needn't handle non-finite values. No bound on the sum of `obs_visible` on one device may be relied on, other than what follows from the above.
Results may differ from the reference program's by a relative error of at most 0.0003.
Values sent between devices are 32-bit elements; how exact they have to be, the bound alone decides.
A program may use at most 128 MiB of HBM per device.

```python
import jax
import jax.numpy as jnp
from jax import lax

S = 1024
P_OBS = 128
EPOCHS = 512


def draw_transition(key, part):
    first_key, second_key, third_key, fourth_key = jax.random.split(key, 4)
    basis, _ = jnp.linalg.qr(jax.random.normal(first_key, (S, S), jnp.float32))
    slow_rate = jnp.exp(jax.random.uniform(second_key, (S,), jnp.float32, jnp.log(0.25 / EPOCHS), jnp.log(1.0 / EPOCHS)))
    fast_rate = jnp.exp(jax.random.uniform(third_key, (S,), jnp.float32, jnp.log(1.0 / 32.0), jnp.log(0.5)))
    share = 0.5
    ranking = jax.random.permutation(fourth_key, S)
    chosen = ranking.astype(jnp.float32) < share * S
    factors = jnp.exp(-jnp.where(chosen, slow_rate, fast_rate))
    matrix = jnp.dot(basis * factors[None, :], basis.T, precision=lax.Precision.HIGHEST)
    return 0.5 * (matrix + matrix.T)


def with_ends(values, key, least, largest):
    place = [jax.random.randint(jax.random.fold_in(key, axis), (), 0, length) for axis, length in enumerate(values.shape)]
    main_axis = values.shape.index(max(values.shape))
    next_to = place[:main_axis] + [(place[main_axis] + 1) % values.shape[main_axis]] + place[main_axis + 1:]
    return values.at[tuple(place)].set(least).at[tuple(next_to)].set(largest)


def block_scale(key, dims, cuts, low, high):
    def one(dim, shards_of):
        heights = jax.random.uniform(jax.random.fold_in(jax.random.fold_in(key, 6), dim), (shards_of,), jnp.float32, low / len(cuts), high / len(cuts))
        return jnp.repeat(jnp.exp(heights), dims[dim] // shards_of).reshape((-1,) + (1,) * (len(dims) - dim - 1))

    level = one(*cuts[0])
    for cut in cuts[1:]:
        level = level * one(*cut)
    return level


def noise(rng, extent, spread, bound, cuts=(), held_as=jnp.bfloat16):
    loudness = block_scale(rng, extent, cuts, -0.22, 0.18) if cuts else 1.0
    values = jax.random.normal(rng, extent, jnp.float32) * spread * loudness
    return jnp.minimum(jnp.maximum(values, -bound), bound).astype(held_as)


def setup_inputs(seed: int = 0) -> dict:
    keys = jax.random.split(jax.random.key(seed), 10)
    return {
        "transition": draw_transition(jax.random.fold_in(keys[9], 71), 0),
        "gain_fwd": noise(keys[1], (S, S), (EPOCHS * P_OBS) ** -0.5, 0.0234375, ((1, 2),), jnp.float32),
        "gain_bwd": noise(keys[2], (S, S), (EPOCHS * P_OBS) ** -0.5, 0.0234375, ((1, 2),), jnp.float32),
        "blend": noise(keys[3], (S, S), S ** -0.5, 0.1875, ((1, 2),), jnp.float32),
        "prior_state": noise(keys[4], (S,), 1.0, 6.0, (), jnp.float32),
        "final_state": noise(keys[5], (S,), 1.0, 6.0, (), jnp.float32),
        "obs_index": with_ends(jax.random.randint(keys[6], (EPOCHS, P_OBS), 0, S), jax.random.fold_in(keys[6], 1), 0, S - 1).astype(jnp.int32),
        "obs_visible": with_ends((jax.random.randint(keys[7], (EPOCHS, P_OBS), 0, 4) < 3).astype(jnp.int32), jax.random.fold_in(keys[7], 1), 0, 1),
        "obs_value": noise(keys[8], (EPOCHS, P_OBS), 1.0, 6.0, ((0, 16),), jnp.float32),
    }


def reference(transition, gain_fwd, gain_bwd, blend, prior_state, final_state, obs_index, obs_visible, obs_value):
    highest = lax.Precision.HIGHEST
    weights = obs_value * obs_visible.astype(jnp.float32)
    places = jnp.broadcast_to(jnp.arange(EPOCHS, dtype=jnp.int32)[:, None], obs_index.shape)
    sparse = jnp.zeros((EPOCHS, S), jnp.float32).at[places, obs_index].add(weights)
    innov_fwd = jnp.dot(sparse, gain_fwd, precision=highest)
    innov_bwd = jnp.dot(sparse, gain_bwd, precision=highest)

    def advance(state_now, innovation):
        nxt = jnp.dot(transition, state_now, precision=highest) + innovation
        return (nxt, nxt)
    _, seq_fwd = lax.scan(advance, prior_state, innov_fwd)
    _, seq_back = lax.scan(advance, final_state, innov_bwd[::-1])
    seq_bwd = seq_back[::-1]
    return seq_fwd + jnp.dot(seq_bwd - seq_fwd, blend, precision=highest)
```

```python
import functools

import jax
import jax.numpy as jnp
from jax import lax
from jax.experimental import pallas as pl
from jax.experimental.pallas import tpu as pltpu
from jax.sharding import PartitionSpec as P

MESH = pl.DeviceIdType.MESH
F32, BF16 = jnp.float32, jnp.bfloat16
LANES = 128


def halves(x):
    high = x.astype(BF16)
    return high, (x - high.astype(F32)).astype(BF16)


def dot(a, b):
    return jnp.dot(a, b, preferred_element_type=F32)


def product(x, w_high, w_low):
    rows = x.shape[0]
    high, low = halves(x)
    both = dot(jnp.concatenate([high, low], axis=0), w_high)
    return both[:rows] + both[rows:] + dot(high, w_low)


def as_rows(ref):
    return jnp.concatenate([ref[:, i, :] for i in range(ref.shape[1])], axis=1)


def kernel(
    segments, levels, tile,
    a_hbm, gf_hbm, gb_hbm, bl_hbm, ends_ref, index_ref, visible_ref, value_ref,
    out_ref,
    a_full, gains, blend, blend_high, blend_low, high, low, sparse, fg, v_in, v_ref,
    f_send, f_all, paths, in_sem, a_send, a_recv, v_send, v_recv, f_send_sem, f_recv_sem,
    x_send, x_recv,
):
    seg = lax.axis_index("tm")
    row = lax.axis_index("row")
    other = 1 - row
    half, size = a_hbm.shape
    epochs = index_ref.shape[0]
    place = seg + row * (segments - 1 - 2 * seg)

    gf_copy = pltpu.make_async_copy(gf_hbm, gains.at[0], in_sem.at[0])
    gb_copy = pltpu.make_async_copy(gb_hbm, gains.at[1], in_sem.at[1])
    bl_copy = pltpu.make_async_copy(bl_hbm, blend, in_sem.at[2])
    own_copy = pltpu.make_async_copy(a_hbm, a_full.at[row], in_sem.at[3])

    barrier = pltpu.get_barrier_semaphore()
    pl.semaphore_signal(barrier, inc=1, device_id=(seg, other), device_id_type=MESH)

    def greet(d, carry):
        pl.semaphore_signal(
            barrier, inc=1, device_id=(lax.rem(seg + d, segments), row), device_id_type=MESH
        )
        return carry

    lax.fori_loop(1, segments, greet, 0)
    gf_copy.start()
    gb_copy.start()
    own_copy.start()
    bl_copy.start()
    pl.semaphore_wait(barrier, segments)

    a_copy = pltpu.make_async_remote_copy(
        src_ref=a_hbm, dst_ref=a_full.at[row], send_sem=a_send, recv_sem=a_recv,
        device_id=(seg, other), device_id_type=MESH,
    )
    a_copy.start()

    groups = size // LANES
    slots = index_ref.shape[1]
    weights = value_ref[...] * visible_ref[...].astype(F32)
    index = index_ref[...]
    group, lane = index // LANES, index % LANES
    group_iota = lax.broadcasted_iota(jnp.int32, (groups, slots), 0)
    lane_iota = lax.broadcasted_iota(jnp.int32, (LANES, slots), 0)
    for k in range(epochs):
        left = jnp.where(group[k : k + 1, :] == group_iota, weights[k : k + 1, :], 0.0)
        right = jnp.where(lane[k : k + 1, :] == lane_iota, 1.0, 0.0).astype(BF16)
        top, mid = halves(left)
        rest = (left - top.astype(F32) - mid.astype(F32)).astype(BF16)
        sums = lax.dot_general(
            jnp.concatenate([top, mid, rest], axis=0), right, (((1,), (1,)), ((), ())),
            preferred_element_type=F32,
        )
        sums = sums[:groups] + sums[groups : 2 * groups] + sums[2 * groups :]
        sparse[0, k] = sums
        sparse[1, epochs - 1 - k] = sums

    gf_copy.wait()
    gb_copy.wait()
    for way in range(2):
        gain_high, gain_low = halves(gains[way])
        fg[way] = product(as_rows(sparse.at[way]), gain_high, gain_low)
    v_copy = pltpu.make_async_remote_copy(
        src_ref=fg.at[other], dst_ref=v_in.at[row], send_sem=v_send, recv_sem=v_recv,
        device_id=(seg, other), device_id_type=MESH,
    )
    v_copy.start()
    v_in[row] = fg[row]

    bl_copy.wait()
    bl_high, bl_low = halves(blend[...])
    blend_high[...] = bl_high
    blend_low[...] = bl_low

    own_copy.wait()
    a_copy.wait_recv()
    for part in range(2):
        diagonal = lax.broadcasted_iota(jnp.int32, (half, size), 1) == (
            lax.broadcasted_iota(jnp.int32, (half, size), 0) + part * half
        )
        first = jnp.where(diagonal, 1.0, 0.0) - a_full[part]
        first_high, first_low = halves(first)
        high[0, part * half : (part + 1) * half, :] = first_high
        low[0, part * half : (part + 1) * half, :] = first_low

    v_copy.wait_recv()
    v_ref[...] = jnp.concatenate([v_in[0], v_in[1]], axis=1)
    epoch_iota = lax.broadcasted_iota(jnp.int32, (epochs, size), 0)

    def send_all(d):
        target = lax.rem(seg + d, segments)
        return pltpu.make_async_remote_copy(
            src_ref=f_send, dst_ref=f_all.at[place + 1],
            send_sem=f_send_sem.at[d], recv_sem=f_recv_sem.at[d],
            device_id=(target, row), device_id_type=MESH,
        )

    def level_step(level, carry):
        step = lax.shift_left(jnp.int32(1), level)
        now = v_ref[...]
        shifted = jnp.where(epoch_iota >= step, pltpu.roll(now, step, 0), 0.0)
        v_ref[...] = now + shifted - product(shifted, high[level], low[level])

        @pl.when(level == levels - 1)
        def _():
            for i in range(groups):
                f_send[i : i + 1, :] = v_ref[epochs - 1 : epochs, i * LANES : (i + 1) * LANES]

            def start(d, c):
                send_all(d).start()
                return c

            lax.fori_loop(1, segments, start, 0)

        for j in range(size // tile):
            columns = slice(j * tile, (j + 1) * tile)
            right_high = high[level, :, columns]
            right_low = low[level, :, columns]
            for i in range(j + 1):
                rows = slice(i * tile, (i + 1) * tile)
                left_high = high[level, rows, :]
                square = (
                    dot(left_high, right_high)
                    + dot(low[level, rows, :], right_high)
                    + dot(left_high, right_low)
                )
                block = high[level, rows, columns].astype(F32) + low[level, rows, columns].astype(F32)
                block = 2.0 * block - square
                block_high, block_low = halves(block)
                high[level + 1, rows, columns] = block_high
                low[level + 1, rows, columns] = block_low
                if i < j:
                    high[level + 1, columns, rows] = block_high.T
                    low[level + 1, columns, rows] = block_low.T
        return carry

    lax.fori_loop(0, levels, level_step, 0)

    def finish(d, carry):
        copy = send_all(d)
        copy.wait_recv()
        copy.wait_send()
        return carry

    lax.fori_loop(1, segments, finish, 0)
    f_all[place + 1] = f_send[...]
    first_state = jnp.where(row == 0, ends_ref[0:1, :], ends_ref[1:2, :])
    for i in range(groups):
        f_all[0, i : i + 1, :] = first_state[:, i * LANES : (i + 1) * LANES]

    def entry(j):
        block = f_all[j]
        return jnp.broadcast_to(
            jnp.concatenate([block[i : i + 1, :] for i in range(groups)], axis=1), (8, size)
        )

    def advance(j, state):
        return state - product(state, high[levels], low[levels]) + entry(j)

    start = lax.fori_loop(1, place + 1, advance, entry(0))

    def spread(level, state):
        chosen = lax.rem(lax.shift_right_logical(epoch_iota + 1, level), 2) == 1
        return jnp.where(chosen, state - product(state, high[level], low[level]), state)

    spread_start = jnp.concatenate([start] * (epochs // 8), axis=0)
    v_ref[...] += lax.fori_loop(0, levels + 1, spread, spread_start)

    for k in range(epochs):
        back = epochs - 1 - k
        paths[row, k : k + 1, :] = jnp.where(row == 0, v_ref[k : k + 1, :], v_ref[back : back + 1, :])
    x_copy = pltpu.make_async_remote_copy(
        src_ref=paths.at[row], dst_ref=paths.at[row], send_sem=x_send, recv_sem=x_recv,
        device_id=(seg, other), device_id_type=MESH,
    )
    x_copy.start()
    own = product(paths[row], blend_high[...], blend_low[...])
    x_copy.wait_recv()
    theirs = product(paths[other], blend_high[...], blend_low[...])
    gap = own - theirs
    mine = paths[0, :, pl.ds(pl.multiple_of(row * half, LANES), half)]
    out_ref[...] = mine + jnp.where(row == 1, gap, -gap)
    x_copy.wait_send()
    v_copy.wait_send()
    a_copy.wait_send()


def per_device(
    segments, transition, gain_fwd, gain_bwd, blend, prior_state, final_state,
    obs_index, obs_visible, obs_value,
):
    half, size = transition.shape
    epochs = obs_index.shape[0]
    levels = (epochs - 1).bit_length()
    groups = size // LANES
    ends = jnp.stack([prior_state, final_state], axis=0)
    anywhere = pl.BlockSpec(memory_space=pl.ANY)
    vmem = pl.BlockSpec(memory_space=pltpu.VMEM)
    dma = pltpu.SemaphoreType.DMA
    return pl.pallas_call(
        functools.partial(kernel, segments, levels, min(256, size)),
        out_shape=jax.ShapeDtypeStruct((epochs, half), F32),
        in_specs=[anywhere] * 4 + [vmem] * 4,
        out_specs=vmem,
        scratch_shapes=[
            pltpu.VMEM((2, half, size), F32),
            pltpu.VMEM((2, size, half), F32),
            pltpu.VMEM((size, half), F32),
            pltpu.VMEM((size, half), BF16),
            pltpu.VMEM((size, half), BF16),
            pltpu.VMEM((levels + 1, size, size), BF16),
            pltpu.VMEM((levels + 1, size, size), BF16),
            pltpu.VMEM((2, epochs, groups, LANES), F32),
            pltpu.VMEM((2, epochs, half), F32),
            pltpu.VMEM((2, epochs, half), F32),
            pltpu.VMEM((epochs, size), F32),
            pltpu.VMEM((groups, LANES), F32),
            pltpu.VMEM((segments + 1, groups, LANES), F32),
            pltpu.VMEM((2, epochs, size), F32),
            dma((4,)), dma, dma, dma, dma, dma((segments,)), dma((segments,)), dma, dma,
        ],
        compiler_params=pltpu.CompilerParams(
            collective_id=0, has_side_effects=True, vmem_limit_bytes=60 * 2**20
        ),
    )(transition, gain_fwd, gain_bwd, blend, ends, obs_index, obs_visible, obs_value)


def solution(mesh):
    placed = (
        P("row", None), P(None, "row"), P(None, "row"), P(None, "row"), P(), P(),
        P("tm", None), P("tm", None), P("tm", None),
    )
    return jax.shard_map(
        functools.partial(per_device, mesh.shape["tm"]),
        mesh=mesh, in_specs=placed, out_specs=P("tm", "row"), check_vma=False,
    )
```

```python
import functools

import jax
import jax.numpy as jnp
from jax import lax
from jax.experimental import pallas as pl
from jax.experimental.pallas import tpu as pltpu
from jax.sharding import PartitionSpec as P

MESH = pl.DeviceIdType.MESH
F32, BF16 = jnp.float32, jnp.bfloat16
LANES = 128


def halves(x):
    high = x.astype(BF16)
    return high, (x - high.astype(F32)).astype(BF16)


def dot(a, b):
    return jnp.dot(a, b, preferred_element_type=F32)


def product(x, w_high, w_low):
    rows = x.shape[0]
    high, low = halves(x)
    both = dot(jnp.concatenate([high, low], axis=0), w_high)
    return both[:rows] + both[rows:] + dot(high, w_low)


def as_rows(ref):
    return jnp.concatenate([ref[:, i, :] for i in range(ref.shape[1])], axis=1)


def kernel(
    segments, levels, tile,
    a_hbm, gf_hbm, gb_hbm, bl_hbm, ends_ref, index_ref, visible_ref, value_ref,
    out_ref,
    a_own, a_other, a_map, gains, blend, blend_high, blend_low, high, low, sparse, fg, v_in, v_ref,
    f_send, f_all, paths, in_sem, a_send, a_recv, v_send, v_recv, f_send_sem, f_recv_sem,
    x_send, x_recv,
):
    seg = lax.axis_index("tm")
    row = lax.axis_index("row")
    other = 1 - row
    half, size = a_hbm.shape
    epochs = index_ref.shape[0]
    place = seg + row * (segments - 1 - 2 * seg)

    gf_copy = pltpu.make_async_copy(gf_hbm, gains.at[0], in_sem.at[0])
    gb_copy = pltpu.make_async_copy(gb_hbm, gains.at[1], in_sem.at[1])
    bl_copy = pltpu.make_async_copy(bl_hbm, blend, in_sem.at[2])
    own_copy = pltpu.make_async_copy(a_hbm, a_own, in_sem.at[3])

    barrier = pltpu.get_barrier_semaphore()
    pl.semaphore_signal(barrier, inc=1, device_id=(seg, other), device_id_type=MESH)

    def greet(d, carry):
        pl.semaphore_signal(
            barrier, inc=1, device_id=(lax.rem(seg + d, segments), row), device_id_type=MESH
        )
        return carry

    lax.fori_loop(1, segments, greet, 0)
    gf_copy.start()
    gb_copy.start()
    own_copy.start()
    bl_copy.start()
    pl.semaphore_wait(barrier, segments)

    own_part = pl.ds(pl.multiple_of(row * half, half), half)
    other_part = pl.ds(pl.multiple_of(other * half, half), half)
    pieces = a_send.shape[0]
    piece = half // pieces
    a_copies = [
        pltpu.make_async_remote_copy(
            src_ref=a_hbm.at[pl.ds(c * piece, piece), own_part],
            dst_ref=a_other.at[pl.ds(c * piece, piece), :],
            send_sem=a_send.at[c], recv_sem=a_recv.at[c],
            device_id=(seg, other), device_id_type=MESH,
        )
        for c in range(pieces)
    ]
    for copy in a_copies:
        copy.start()

    groups = size // LANES
    slots = index_ref.shape[1]
    weights = value_ref[...] * visible_ref[...].astype(F32)
    index = index_ref[...]
    group, lane = index // LANES, index % LANES
    group_iota = lax.broadcasted_iota(jnp.int32, (groups, slots), 0)
    lane_iota = lax.broadcasted_iota(jnp.int32, (LANES, slots), 0)
    for k in range(epochs):
        left = jnp.where(group[k : k + 1, :] == group_iota, weights[k : k + 1, :], 0.0)
        right = jnp.where(lane[k : k + 1, :] == lane_iota, 1.0, 0.0).astype(BF16)
        top, mid = halves(left)
        rest = (left - top.astype(F32) - mid.astype(F32)).astype(BF16)
        sums = lax.dot_general(
            jnp.concatenate([top, mid, rest], axis=0), right, (((1,), (1,)), ((), ())),
            preferred_element_type=F32,
        )
        sums = sums[:groups] + sums[groups : 2 * groups] + sums[2 * groups :]
        sparse[0, k] = sums
        sparse[1, epochs - 1 - k] = sums

    gf_copy.wait()
    gb_copy.wait()
    for way in range(2):
        gain_high, gain_low = halves(gains[way])
        fg[way] = product(as_rows(sparse.at[way]), gain_high, gain_low)
    v_copy = pltpu.make_async_remote_copy(
        src_ref=fg.at[other], dst_ref=v_in.at[row], send_sem=v_send, recv_sem=v_recv,
        device_id=(seg, other), device_id_type=MESH,
    )
    v_copy.start()
    v_in[row] = fg[row]

    bl_copy.wait()
    bl_high, bl_low = halves(blend[...])
    blend_high[...] = bl_high
    blend_low[...] = bl_low

    own_copy.wait()
    identity = jnp.where(
        lax.broadcasted_iota(jnp.int32, (half, half), 0)
        == lax.broadcasted_iota(jnp.int32, (half, half), 1), 1.0, 0.0,
    )
    block_high, block_low = halves(identity - a_own[:, own_part])
    high[0, own_part, own_part] = block_high
    low[0, own_part, own_part] = block_low
    block_high, block_low = halves(-a_own[:, other_part])
    high[0, own_part, other_part] = block_high
    low[0, own_part, other_part] = block_low
    high[0, other_part, own_part] = block_high.T
    low[0, other_part, own_part] = block_low.T
    for copy in a_copies:
        copy.wait_recv()
    block_high, block_low = halves(identity - a_other[...])
    high[0, other_part, other_part] = block_high
    low[0, other_part, other_part] = block_low

    v_copy.wait_recv()
    v_ref[...] = jnp.concatenate([v_in[0], v_in[1]], axis=1)
    epoch_iota = lax.broadcasted_iota(jnp.int32, (epochs, size), 0)

    def send_all(d):
        target = lax.rem(seg + d, segments)
        return pltpu.make_async_remote_copy(
            src_ref=f_send, dst_ref=f_all.at[place + 1],
            send_sem=f_send_sem.at[d], recv_sem=f_recv_sem.at[d],
            device_id=(target, row), device_id_type=MESH,
        )

    def level_step(level, carry):
        step = lax.shift_left(jnp.int32(1), level)
        now = v_ref[...]
        shifted = jnp.where(epoch_iota >= step, pltpu.roll(now, step, 0), 0.0)
        v_ref[...] = now + shifted - product(shifted, high[level], low[level])

        @pl.when(level == levels - 1)
        def _():
            for i in range(groups):
                f_send[i : i + 1, :] = v_ref[epochs - 1 : epochs, i * LANES : (i + 1) * LANES]

            def start(d, c):
                send_all(d).start()
                return c

            lax.fori_loop(1, segments, start, 0)

        @pl.when(level < levels - 1)
        def _():
            for j in range(size // tile):
                columns = slice(j * tile, (j + 1) * tile)
                right_high = high[level, :, columns]
                right_low = low[level, :, columns]
                upper = slice(0, (j + 1) * tile)
                left_high = high[level, upper, :]
                square = (
                    dot(left_high, right_high)
                    + dot(low[level, upper, :], right_high)
                    + dot(left_high, right_low)
                )
                block = high[level, upper, columns].astype(F32) + low[level, upper, columns].astype(F32)
                block = 2.0 * block - square
                block_high, block_low = halves(block)
                high[level + 1, upper, columns] = block_high
                low[level + 1, upper, columns] = block_low
                if j > 0:
                    high[level + 1, columns, : j * tile] = block_high[: j * tile].T
                    low[level + 1, columns, : j * tile] = block_low[: j * tile].T

        return carry

    lax.fori_loop(0, levels, level_step, 0)

    for i in range(size // tile):
        rows = slice(i * tile, (i + 1) * tile)
        diagonal = lax.broadcasted_iota(jnp.int32, (tile, size), 1) == (
            lax.broadcasted_iota(jnp.int32, (tile, size), 0) + i * tile
        )
        a_map[rows, :] = (
            jnp.where(diagonal, 1.0, 0.0) - high[levels - 1, rows, :].astype(F32)
        ) - low[levels - 1, rows, :].astype(F32)

    def finish(d, carry):
        copy = send_all(d)
        copy.wait_recv()
        copy.wait_send()
        return carry

    lax.fori_loop(1, segments, finish, 0)
    f_all[place + 1] = f_send[...]
    first_state = jnp.where(row == 0, ends_ref[0:1, :], ends_ref[1:2, :])
    for i in range(groups):
        f_all[0, i : i + 1, :] = first_state[:, i * LANES : (i + 1) * LANES]

    def entry(j):
        block = f_all[j]
        return jnp.broadcast_to(
            jnp.concatenate([block[i : i + 1, :] for i in range(groups)], axis=1), (8, size)
        )

    chunk = 32

    def advance(j, state):
        total = jnp.zeros((8, size), F32)
        for i in range(size // chunk):
            rows = a_map[i * chunk : (i + 1) * chunk, :]
            dots = jnp.sum(
                (rows.reshape(chunk // 8, 8, size) * state[None]).reshape(chunk, size),
                axis=1, keepdims=True,
            )
            total = total + jnp.sum((rows * dots).reshape(chunk // 8, 8, size), axis=0)
        return jnp.broadcast_to(jnp.sum(total, axis=0, keepdims=True), (8, size)) + entry(j)

    start = lax.fori_loop(1, place + 1, advance, entry(0))

    turns = epoch_iota + 1
    turns = jnp.where(turns == epochs, epochs + epochs // 2, turns)

    def spread(level, state):
        power = jnp.minimum(level, levels - 1)
        chosen = lax.rem(lax.shift_right_logical(turns, level), 2) == 1
        return jnp.where(chosen, state - product(state, high[power], low[power]), state)

    spread_start = jnp.concatenate([start] * (epochs // 8), axis=0)
    v_ref[...] += lax.fori_loop(0, levels + 1, spread, spread_start)

    for k in range(epochs):
        back = epochs - 1 - k
        paths[row, k : k + 1, :] = jnp.where(row == 0, v_ref[k : k + 1, :], v_ref[back : back + 1, :])
    x_copy = pltpu.make_async_remote_copy(
        src_ref=paths.at[row], dst_ref=paths.at[row], send_sem=x_send, recv_sem=x_recv,
        device_id=(seg, other), device_id_type=MESH,
    )
    x_copy.start()
    own = product(paths[row], blend_high[...], blend_low[...])
    x_copy.wait_recv()
    theirs = product(paths[other], blend_high[...], blend_low[...])
    gap = own - theirs
    mine = paths[0, :, pl.ds(pl.multiple_of(row * half, LANES), half)]
    out_ref[...] = mine + jnp.where(row == 1, gap, -gap)
    x_copy.wait_send()
    v_copy.wait_send()
    for copy in a_copies:
        copy.wait_send()


def per_device(
    segments, transition, gain_fwd, gain_bwd, blend, prior_state, final_state,
    obs_index, obs_visible, obs_value,
):
    half, size = transition.shape
    epochs = obs_index.shape[0]
    levels = (epochs - 1).bit_length()
    groups = size // LANES
    ends = jnp.stack([prior_state, final_state], axis=0)
    anywhere = pl.BlockSpec(memory_space=pl.ANY)
    vmem = pl.BlockSpec(memory_space=pltpu.VMEM)
    dma = pltpu.SemaphoreType.DMA
    return pl.pallas_call(
        functools.partial(kernel, segments, levels, min(256, size)),
        out_shape=jax.ShapeDtypeStruct((epochs, half), F32),
        in_specs=[anywhere] * 4 + [vmem] * 4,
        out_specs=vmem,
        scratch_shapes=[
            pltpu.VMEM((half, size), F32),
            pltpu.VMEM((half, half), F32),
            pltpu.VMEM((size, size), F32),
            pltpu.VMEM((2, size, half), F32),
            pltpu.VMEM((size, half), F32),
            pltpu.VMEM((size, half), BF16),
            pltpu.VMEM((size, half), BF16),
            pltpu.VMEM((levels, size, size), BF16),
            pltpu.VMEM((levels, size, size), BF16),
            pltpu.VMEM((2, epochs, groups, LANES), F32),
            pltpu.VMEM((2, epochs, half), F32),
            pltpu.VMEM((2, epochs, half), F32),
            pltpu.VMEM((epochs, size), F32),
            pltpu.VMEM((groups, LANES), F32),
            pltpu.VMEM((segments + 1, groups, LANES), F32),
            pltpu.VMEM((2, epochs, size), F32),
            dma((4,)), dma((4,)), dma((4,)), dma, dma, dma((segments,)), dma((segments,)), dma, dma,
        ],
        compiler_params=pltpu.CompilerParams(
            collective_id=0, has_side_effects=True, vmem_limit_bytes=60 * 2**20
        ),
    )(transition, gain_fwd, gain_bwd, blend, ends, obs_index, obs_visible, obs_value)


def solution(mesh):
    placed = (
        P("row", None), P(None, "row"), P(None, "row"), P(None, "row"), P(), P(),
        P("tm", None), P("tm", None), P("tm", None),
    )
    return jax.shard_map(
        functools.partial(per_device, mesh.shape["tm"]),
        mesh=mesh, in_specs=placed, out_specs=P("tm", "row"), check_vma=False,
    )
```

```python
import functools

import jax
import jax.numpy as jnp
from jax import lax
from jax.experimental import pallas as pl
from jax.experimental.pallas import tpu as pltpu
from jax.sharding import PartitionSpec as P

MESH = pl.DeviceIdType.MESH
F32, BF16 = jnp.float32, jnp.bfloat16
LANES = 128


def halves(x):
    high = x.astype(BF16)
    return high, (x - high.astype(F32)).astype(BF16)


def dot(a, b):
    return jnp.dot(a, b, preferred_element_type=F32)


def product(x, w_high, w_low):
    rows = x.shape[0]
    high, low = halves(x)
    both = dot(jnp.concatenate([high, low], axis=0), w_high)
    return both[:rows] + both[rows:] + dot(high, w_low)


def as_rows(ref):
    return jnp.concatenate([ref[:, i, :] for i in range(ref.shape[1])], axis=1)


def kernel(
    segments, levels, tile,
    a_hbm, gf_hbm, gb_hbm, bl_hbm, ends_ref, index_ref, visible_ref, value_ref,
    out_ref,
    a_own, a_other, a_map, gains, blend, blend_high, blend_low, high, low, sparse, fg, v_in, v_ref,
    f_send, f_all, paths, in_sem, a_send, a_recv, v_send, v_recv, f_send_sem, f_recv_sem,
    x_send, x_recv,
):
    seg = lax.axis_index("tm")
    row = lax.axis_index("row")
    other = 1 - row
    half, size = a_hbm.shape
    epochs = index_ref.shape[0]
    place = seg + row * (segments - 1 - 2 * seg)

    gf_copy = pltpu.make_async_copy(gf_hbm, gains.at[0], in_sem.at[0])
    gb_copy = pltpu.make_async_copy(gb_hbm, gains.at[1], in_sem.at[1])
    bl_copy = pltpu.make_async_copy(bl_hbm, blend, in_sem.at[2])
    own_copy = pltpu.make_async_copy(a_hbm, a_own, in_sem.at[3])

    barrier = pltpu.get_barrier_semaphore()
    pl.semaphore_signal(barrier, inc=1, device_id=(seg, other), device_id_type=MESH)

    def greet(d, carry):
        pl.semaphore_signal(
            barrier, inc=1, device_id=(lax.rem(seg + d, segments), row), device_id_type=MESH
        )
        return carry

    lax.fori_loop(1, segments, greet, 0)
    gf_copy.start()
    gb_copy.start()
    own_copy.start()
    bl_copy.start()
    pl.semaphore_wait(barrier, segments)

    own_part = pl.ds(pl.multiple_of(row * half, half), half)
    other_part = pl.ds(pl.multiple_of(other * half, half), half)
    pieces = a_send.shape[0]
    piece = half // pieces
    a_copies = [
        pltpu.make_async_remote_copy(
            src_ref=a_hbm.at[pl.ds(c * piece, piece), own_part],
            dst_ref=a_other.at[pl.ds(c * piece, piece), :],
            send_sem=a_send.at[c], recv_sem=a_recv.at[c],
            device_id=(seg, other), device_id_type=MESH,
        )
        for c in range(pieces)
    ]
    for copy in a_copies:
        copy.start()

    groups = size // LANES
    slots = index_ref.shape[1]
    weights = value_ref[...] * visible_ref[...].astype(F32)
    index = index_ref[...]
    group, lane = index // LANES, index % LANES
    group_iota = lax.broadcasted_iota(jnp.int32, (groups, slots), 0)
    lane_iota = lax.broadcasted_iota(jnp.int32, (LANES, slots), 0)
    for k in range(epochs):
        left = jnp.where(group[k : k + 1, :] == group_iota, weights[k : k + 1, :], 0.0)
        right = jnp.where(lane[k : k + 1, :] == lane_iota, 1.0, 0.0).astype(BF16)
        top, mid = halves(left)
        rest = (left - top.astype(F32) - mid.astype(F32)).astype(BF16)
        sums = lax.dot_general(
            jnp.concatenate([top, mid, rest], axis=0), right, (((1,), (1,)), ((), ())),
            preferred_element_type=F32,
        )
        sums = sums[:groups] + sums[groups : 2 * groups] + sums[2 * groups :]
        sparse[0, k] = sums
        sparse[1, epochs - 1 - k] = sums

    gf_copy.wait()
    gb_copy.wait()
    for way in range(2):
        gain_high, gain_low = halves(gains[way])
        fg[way] = product(as_rows(sparse.at[way]), gain_high, gain_low)
    v_copy = pltpu.make_async_remote_copy(
        src_ref=fg.at[other], dst_ref=v_in.at[row], send_sem=v_send, recv_sem=v_recv,
        device_id=(seg, other), device_id_type=MESH,
    )
    v_copy.start()
    v_in[row] = fg[row]

    bl_copy.wait()
    bl_high, bl_low = halves(blend[...])
    blend_high[...] = bl_high
    blend_low[...] = bl_low

    own_copy.wait()
    identity = jnp.where(
        lax.broadcasted_iota(jnp.int32, (half, half), 0)
        == lax.broadcasted_iota(jnp.int32, (half, half), 1), 1.0, 0.0,
    )
    block_high, block_low = halves(identity - a_own[:, own_part])
    high[0, own_part, own_part] = block_high
    low[0, own_part, own_part] = block_low
    block_high, block_low = halves(-a_own[:, other_part])
    high[0, own_part, other_part] = block_high
    low[0, own_part, other_part] = block_low
    high[0, other_part, own_part] = block_high.T
    low[0, other_part, own_part] = block_low.T
    for copy in a_copies:
        copy.wait_recv()
    block_high, block_low = halves(identity - a_other[...])
    high[0, other_part, other_part] = block_high
    low[0, other_part, other_part] = block_low

    v_copy.wait_recv()
    v_ref[...] = jnp.concatenate([v_in[0], v_in[1]], axis=1)
    epoch_iota = lax.broadcasted_iota(jnp.int32, (epochs, size), 0)

    def send_all(d):
        target = lax.rem(seg + d, segments)
        return pltpu.make_async_remote_copy(
            src_ref=f_send, dst_ref=f_all.at[place + 1],
            send_sem=f_send_sem.at[d], recv_sem=f_recv_sem.at[d],
            device_id=(target, row), device_id_type=MESH,
        )

    def level_step(level, carry):
        step = lax.shift_left(jnp.int32(1), level)
        now = v_ref[...]
        shifted = jnp.where(epoch_iota >= step, pltpu.roll(now, step, 0), 0.0)
        shift_high, shift_low = halves(shifted)

        @pl.when(level == levels - 1)
        def _():
            v_ref[...] = now + shifted - product(shifted, high[level], low[level])
            for i in range(groups):
                f_send[i : i + 1, :] = v_ref[epochs - 1 : epochs, i * LANES : (i + 1) * LANES]

            def start(d, c):
                send_all(d).start()
                return c

            lax.fori_loop(1, segments, start, 0)

        @pl.when(level < levels - 1)
        def _():
            for j in range(size // tile):
                columns = slice(j * tile, (j + 1) * tile)
                right_high = high[level, :, columns]
                right_low = low[level, :, columns]
                upper = slice(0, (j + 1) * tile)
                left_high = high[level, upper, :]
                by_high = dot(jnp.concatenate([shift_high, shift_low, left_high], axis=0), right_high)
                by_low = dot(jnp.concatenate([shift_high, left_high], axis=0), right_low)
                v_ref[:, columns] = (now[:, columns] + shifted[:, columns]) - (
                    by_high[:epochs] + by_high[epochs : 2 * epochs] + by_low[:epochs]
                )
                square = by_high[2 * epochs :] + dot(low[level, upper, :], right_high) + by_low[epochs:]
                block = high[level, upper, columns].astype(F32) + low[level, upper, columns].astype(F32)
                block = 2.0 * block - square
                block_high, block_low = halves(block)
                high[level + 1, upper, columns] = block_high
                low[level + 1, upper, columns] = block_low
                if j > 0:
                    high[level + 1, columns, : j * tile] = block_high[: j * tile].T
                    low[level + 1, columns, : j * tile] = block_low[: j * tile].T

        return carry

    lax.fori_loop(0, levels, level_step, 0)

    for i in range(size // tile):
        rows = slice(i * tile, (i + 1) * tile)
        diagonal = lax.broadcasted_iota(jnp.int32, (tile, size), 1) == (
            lax.broadcasted_iota(jnp.int32, (tile, size), 0) + i * tile
        )
        a_map[rows, :] = (
            jnp.where(diagonal, 1.0, 0.0) - high[levels - 1, rows, :].astype(F32)
        ) - low[levels - 1, rows, :].astype(F32)

    def finish(d, carry):
        copy = send_all(d)
        copy.wait_recv()
        copy.wait_send()
        return carry

    lax.fori_loop(1, segments, finish, 0)
    f_all[place + 1] = f_send[...]
    first_state = jnp.where(row == 0, ends_ref[0:1, :], ends_ref[1:2, :])
    for i in range(groups):
        f_all[0, i : i + 1, :] = first_state[:, i * LANES : (i + 1) * LANES]

    def entry(j):
        block = f_all[j]
        return jnp.broadcast_to(
            jnp.concatenate([block[i : i + 1, :] for i in range(groups)], axis=1), (8, size)
        )

    chunk = 32

    def two_steps(state):
        total = jnp.zeros((8, size), F32)
        for i in range(size // chunk):
            rows = a_map[i * chunk : (i + 1) * chunk, :]
            dots = jnp.sum(
                (rows.reshape(chunk // 8, 8, size) * state[None]).reshape(chunk, size),
                axis=1, keepdims=True,
            )
            total = total + jnp.sum((rows * dots).reshape(chunk // 8, 8, size), axis=0)
        return jnp.broadcast_to(jnp.sum(total, axis=0, keepdims=True), (8, size))

    def advance(j, state):
        return two_steps(state) + entry(j)

    start = lax.fori_loop(1, place + 1, advance, entry(0))

    def spread(level, state):
        chosen = lax.rem(lax.shift_right_logical(epoch_iota + 1, level), 2) == 1
        return jnp.where(chosen, state - product(state, high[level], low[level]), state)

    spread_start = jnp.concatenate([start] * (epochs // 8), axis=0)
    through = jnp.concatenate([two_steps(start)] * (epochs // 8), axis=0)
    within = lax.fori_loop(0, levels, spread, spread_start)
    v_ref[...] += jnp.where(epoch_iota == epochs - 1, through, within)

    for k in range(epochs):
        back = epochs - 1 - k
        paths[row, k : k + 1, :] = jnp.where(row == 0, v_ref[k : k + 1, :], v_ref[back : back + 1, :])
    x_copy = pltpu.make_async_remote_copy(
        src_ref=paths.at[row], dst_ref=paths.at[row], send_sem=x_send, recv_sem=x_recv,
        device_id=(seg, other), device_id_type=MESH,
    )
    x_copy.start()
    own = product(paths[row], blend_high[...], blend_low[...])
    x_copy.wait_recv()
    theirs = product(paths[other], blend_high[...], blend_low[...])
    gap = own - theirs
    mine = paths[0, :, pl.ds(pl.multiple_of(row * half, LANES), half)]
    out_ref[...] = mine + jnp.where(row == 1, gap, -gap)
    x_copy.wait_send()
    v_copy.wait_send()
    for copy in a_copies:
        copy.wait_send()


def per_device(
    segments, transition, gain_fwd, gain_bwd, blend, prior_state, final_state,
    obs_index, obs_visible, obs_value,
):
    half, size = transition.shape
    epochs = obs_index.shape[0]
    levels = (epochs - 1).bit_length()
    groups = size // LANES
    ends = jnp.stack([prior_state, final_state], axis=0)
    anywhere = pl.BlockSpec(memory_space=pl.ANY)
    vmem = pl.BlockSpec(memory_space=pltpu.VMEM)
    dma = pltpu.SemaphoreType.DMA
    return pl.pallas_call(
        functools.partial(kernel, segments, levels, min(256, size)),
        out_shape=jax.ShapeDtypeStruct((epochs, half), F32),
        in_specs=[anywhere] * 4 + [vmem] * 4,
        out_specs=vmem,
        scratch_shapes=[
            pltpu.VMEM((half, size), F32),
            pltpu.VMEM((half, half), F32),
            pltpu.VMEM((size, size), F32),
            pltpu.VMEM((2, size, half), F32),
            pltpu.VMEM((size, half), F32),
            pltpu.VMEM((size, half), BF16),
            pltpu.VMEM((size, half), BF16),
            pltpu.VMEM((levels, size, size), BF16),
            pltpu.VMEM((levels, size, size), BF16),
            pltpu.VMEM((2, epochs, groups, LANES), F32),
            pltpu.VMEM((2, epochs, half), F32),
            pltpu.VMEM((2, epochs, half), F32),
            pltpu.VMEM((epochs, size), F32),
            pltpu.VMEM((groups, LANES), F32),
            pltpu.VMEM((segments + 1, groups, LANES), F32),
            pltpu.VMEM((2, epochs, size), F32),
            dma((4,)), dma((4,)), dma((4,)), dma, dma, dma((segments,)), dma((segments,)), dma, dma,
        ],
        compiler_params=pltpu.CompilerParams(
            collective_id=0, has_side_effects=True, vmem_limit_bytes=60 * 2**20
        ),
    )(transition, gain_fwd, gain_bwd, blend, ends, obs_index, obs_visible, obs_value)


def solution(mesh):
    placed = (
        P("row", None), P(None, "row"), P(None, "row"), P(None, "row"), P(), P(),
        P("tm", None), P("tm", None), P("tm", None),
    )
    return jax.shard_map(
        functools.partial(per_device, mesh.shape["tm"]),
        mesh=mesh, in_specs=placed, out_specs=P("tm", "row"), check_vma=False,
    )
```
